32 devices in a mesh: expert: 8 (over z, y), shard: 4 (over x, core).
Axes of the slice: x: 2, y: 2, z: 4, core: 2. Of those that a mesh axis runs over, the one named last changes fastest.
Arguments:
- tokens: bfloat16 [16384, 768], P(('expert', 'shard')), may hold values from -6 to 6
- segment_ids: int32 [16384], P(('expert', 'shard')), may hold values from 0 to 1, as said below
- routes: int32 [16384], P(('expert', 'shard')), may hold values from 0 to 7, as said below
- slots: int32 [16384], P(('expert', 'shard')), may hold values from 0 to 127, as said below
- qkv_weight: bfloat16 [768, 2304], P('shard'), may hold values from -0.21875 to 0.21875
- out_weight: bfloat16 [768, 768], P('shard'), may hold values from -1.25 to 1.25
- bias_table: float32 [32, 12], replicated, may hold values from -4 to 4
- norm_gain: float32 [768], replicated, may hold values from 0.1 to 1.9
- ffn_gain: float32 [768], replicated, may hold values from 0.1 to 1.9
- router_weight: float32 [768, 8], replicated, may hold values from -0.15625 to 0.15625
- expert_in: bfloat16 [8, 768, 3072], P('expert'), may hold values from -0.21875 to 0.21875
- expert_out: bfloat16 [8, 3072, 768], P('expert'), may hold values from -0.875 to 0.875
- cotangent: bfloat16 [16384, 768], P(('expert', 'shard')), may hold values from -6 to 6
Outputs:
- layer_out: float32 [16384, 768], P(('expert', 'shard'))
- grad_tokens: float32 [16384, 768], P(('expert', 'shard'))
- grad_qkv: float32 [768, 2304], P(('expert', 'shard'))
- grad_out_weight: float32 [768, 768], P(('expert', 'shard'))
- grad_bias_table: float32 [32, 12], replicated
- grad_norm_gain: float32 [768], replicated
- grad_ffn_gain: float32 [768], replicated
- grad_router: float32 [768, 8], replicated
- grad_expert_in: float32 [8, 768, 3072], P('expert', 'shard')
- grad_expert_out: float32 [8, 3072, 768], P('expert', 'shard')
The draws below stay inside these ranges and needn't reach their ends.
Inputs may be any that keep to these rules, and one draw needn't show every extreme that they name: `segment_ids`: segment numbers within one device's 512 rows never fall; every number 0 to 1 occurs on every device. `routes`: within one device's 512 rows no expert is named more than 128 times; some expert is named exactly 128 times by every device. Tokens of one device that name the same expert have different slots.
All inputs are finite; a program needn't handle non-finite values.
Results may differ from the reference program's by a relative error of at most 0.014.
Values may be sent and summed in bfloat16 or wider, within the bound.
A program may use at most 192 MiB of HBM per device.

```python
import math
import jax
import jax.numpy as jnp
from jax import lax

D = 768
HEADS = 12
HEAD = 64
FF = 3072
BUCKETS = 32
MAXDIST = 128
TOK_DEV = 512
EXPERTS = 8
CAP = 128
SEGS = 2
GROUPS = 32
TOKENS = 16384


def draw_segment_ids(key, part):
    key = jax.random.fold_in(key, 11)
    group_keys = jax.random.split(key, GROUPS)

    def one_group(group_key):
        cut_points = jnp.sort(jax.random.permutation(group_key, TOK_DEV - 1)[:SEGS - 1] + 1)
        positions = jnp.arange(TOK_DEV)
        return jnp.sum(positions[:, None] >= cut_points[None, :], axis=1).astype(jnp.int32)
    return jax.vmap(one_group)(group_keys).reshape(TOKENS)


def route_cells(key):
    cell_count = EXPERTS * CAP
    full_expert = jax.random.randint(jax.random.fold_in(key, 5), (), 0, EXPERTS)
    group_keys = jax.random.split(jax.random.fold_in(key, 6), GROUPS)
    cell_expert = jnp.arange(cell_count) // CAP

    def one_group(group_key):
        rank_key, offset_key, order_key = jax.random.split(group_key, 3)
        ranking = jax.random.permutation(rank_key, cell_count)
        offsets = jax.random.randint(offset_key, (EXPERTS,), 0, cell_count)
        scored = (ranking + offsets[cell_expert]) * cell_count + ranking
        scored = jnp.where(cell_expert == full_expert, ranking - cell_count, scored)
        picked = jnp.argsort(scored)[:TOK_DEV]
        return jax.random.permutation(order_key, picked)
    return jax.vmap(one_group)(group_keys).reshape(TOKENS)


def draw_routes(key, part):
    return (route_cells(key) // CAP).astype(jnp.int32)


def draw_slots(key, part):
    return (route_cells(key) % CAP).astype(jnp.int32)


def block_levels(stream_key, shape, cuts, low, top_value):
    def one(axis_at, blocks):
        steps = jax.random.uniform(jax.random.fold_in(jax.random.fold_in(stream_key, 6), axis_at), (blocks,), jnp.float32, low / len(cuts), top_value / len(cuts))
        return jnp.repeat(jnp.exp(steps), shape[axis_at] // blocks).reshape((-1,) + (1,) * (len(shape) - axis_at - 1))

    loudness = one(*cuts[0])
    for cut in cuts[1:]:
        loudness = loudness * one(*cut)
    return loudness


def noise(key, extent, spread, most, cuts=(), dtype=jnp.bfloat16):
    drawn = jax.random.normal(key, extent, jnp.float32) * spread
    if len(cuts) > 0:
        drawn = block_levels(key, extent, cuts, -0.22, 0.18) * drawn
    return jnp.clip(drawn, min=-most, max=most).astype(dtype)


def setup_inputs(seed: int = 0) -> dict:
    keys = jax.random.split(jax.random.key(seed), 14)
    tokens = noise(keys[0], (TOKENS, D), 1.0, 6.0, ((0, 32),))
    segment_ids = draw_segment_ids(jax.random.fold_in(keys[13], 71), 0)
    routes = draw_routes(jax.random.fold_in(keys[13], 71), 0)
    slots = draw_slots(jax.random.fold_in(keys[13], 71), 0)
    qkv_weight = noise(keys[4], (D, 3 * D), D ** -0.5, 0.21875, ((0, 4),))
    out_weight = noise(keys[5], (D, D), (D // 32) ** -0.5, 1.25, ((0, 4),))
    bias_table = noise(keys[6], (BUCKETS, HEADS), 1.0, 4.0, (), jnp.float32)
    norm_gain = jnp.clip(1.0 + 0.18 * jax.random.normal(keys[7], (D,), jnp.float32), 0.1, 1.9)
    ffn_gain = jnp.clip(1.0 + 0.18 * jax.random.normal(keys[8], (D,), jnp.float32), 0.1, 1.9)
    router_weight = noise(keys[9], (D, EXPERTS), (2 * D) ** -0.5, 0.15625, (), jnp.float32)
    expert_in = noise(keys[10], (EXPERTS, D, FF), D ** -0.5, 0.21875, ((0, 8),))
    expert_out = noise(keys[11], (EXPERTS, FF, D), (max(1, FF // (EXPERTS * EXPERTS))) ** -0.5, 0.875, ((0, 8),))
    cotangent = noise(keys[12], (TOKENS, D), 1.0, 6.0, ((0, 32),))
    return {"tokens": tokens, "segment_ids": segment_ids, "routes": routes, "slots": slots, "qkv_weight": qkv_weight, "out_weight": out_weight, "bias_table": bias_table, "norm_gain": norm_gain, "ffn_gain": ffn_gain, "router_weight": router_weight, "expert_in": expert_in, "expert_out": expert_out, "cotangent": cotangent}


@jax.custom_vjp
def low(v):
    return lax.optimization_barrier(v.astype(jnp.bfloat16)).astype(jnp.float32)

@jax.custom_vjp
def low_back(v):
    return v

def low_keep(v):
    return (low(v), None)

def low_pass(kept, grad):
    return (grad,)

def back_keep(v):
    return (v, None)

def back_low(kept, grad):
    return (low(grad),)
low.defvjp(low_keep, low_pass)
low_back.defvjp(back_keep, back_low)
epsilon = 1e-06
neg_large = -1e+30
highest = lax.Precision.HIGHEST

def thresholds(buckets, farthest):
    exact_count = buckets // 4
    return [math.ceil(exact_count * (farthest / exact_count) ** (tier_index / exact_count)) for tier_index in range(1, exact_count)]

def bucket_of(distance, buckets, farthest):
    exact_count = buckets // 4
    magnitude = jnp.abs(distance)
    beyond = exact_count + sum(((magnitude >= edge_value).astype(jnp.int32) for edge_value in thresholds(buckets, farthest)))
    near_far = jnp.where(magnitude < exact_count, magnitude, beyond)
    return (jnp.where(distance > 0, 2 * exact_count, 0) + near_far).astype(jnp.int32)

def rms_norm(values, gain):
    return values * lax.rsqrt(lax.optimization_barrier(jnp.mean(values * values, axis=-1, keepdims=True)) + epsilon) * gain

def reference(tokens, segment_ids, routes, slots, qkv_weight, out_weight, bias_table, norm_gain, ffn_gain, router_weight, expert_in, expert_out, cotangent):
    local_pos = jnp.arange(TOK_DEV)
    bucket_grid = bucket_of(local_pos[None, :] - local_pos[:, None], BUCKETS, MAXDIST)
    seg_groups = segment_ids.reshape(GROUPS, TOK_DEV)
    group_ids = (jnp.arange(TOKENS) // TOK_DEV).astype(jnp.int32)
    dest_rows = (group_ids * CAP + slots).astype(jnp.int32)
    expert_ids = jnp.arange(EXPERTS).astype(jnp.int32)

    def forward(token_vals, qkv_vals, out_vals, table, gain_one, gain_two, router_vals, inner_weights, outer_weights):
        normed = rms_norm(token_vals, gain_one)
        packed = low_back(low(jnp.dot(low(normed), qkv_vals, precision=highest)))
        grouped = packed.reshape(GROUPS, TOK_DEV, 3, HEADS, HEAD)
        bias_grid = jnp.transpose(table[bucket_grid], (2, 0, 1))

        def attend(pieces):
            block_qkv, seg_row = pieces
            scores = jnp.einsum('qhd,khd->hqk', block_qkv[:, 0], block_qkv[:, 1], precision=highest) * 0.125 + bias_grid
            scores = low_back(scores)
            allowed = (seg_row[:, None] == seg_row[None, :])[None]
            weights_soft = jax.nn.softmax(jnp.where(allowed, scores, neg_large), axis=-1)
            mixed = jnp.einsum('hqk,khd->qhd', low(weights_soft), block_qkv[:, 2], precision=highest)
            return mixed.reshape(TOK_DEV, D)
        attended = lax.map(jax.checkpoint(attend), (grouped, seg_groups))
        attended = low_back(low(attended.reshape(TOKENS, D)))
        branch = low_back(jnp.dot(attended, out_vals, precision=highest))
        middle = token_vals + branch
        normed_two = rms_norm(middle, gain_two)
        logits = jnp.dot(normed_two, router_vals, precision=highest)
        router_probs = jax.nn.softmax(logits, axis=-1)
        chosen = routes[:, None] == expert_ids[None, :]
        gates = lax.optimization_barrier(jnp.sum(jnp.where(chosen, router_probs, 0.0), axis=-1))
        sent = low_back(low(normed_two))

        def expert_step(running, pieces):
            expert_index, weight_in, weight_out = pieces
            picked = routes == expert_index
            target_rows = jnp.where(picked, dest_rows, GROUPS * CAP).astype(jnp.int32)
            buffer = jnp.zeros((GROUPS * CAP + 1, D), jnp.float32).at[target_rows].add(jnp.where(picked[:, None], sent, 0.0))
            inner_raw = low_back(jnp.dot(buffer, weight_in, precision=highest))
            activated = low(jax.nn.gelu(inner_raw, approximate=False))
            returned = low_back(low(jnp.dot(activated, weight_out, precision=highest)))
            return (running + jnp.where(picked[:, None], returned[target_rows], 0.0), None)
        combined = lax.scan(jax.checkpoint(expert_step), jnp.zeros((TOKENS, D), jnp.float32), (expert_ids, inner_weights, outer_weights))[0]
        return middle + gates[:, None] * combined
    inputs = (tokens.astype(jnp.float32), qkv_weight.astype(jnp.float32), out_weight.astype(jnp.float32), bias_table, norm_gain, ffn_gain, router_weight, expert_in.astype(jnp.float32), expert_out.astype(jnp.float32))
    layer_value, pullback = jax.vjp(forward, *inputs)
    gradients = pullback(cotangent.astype(jnp.float32))
    return (layer_value, gradients[0], gradients[1], gradients[2], gradients[3], gradients[4], gradients[5], gradients[6], gradients[7], gradients[8])
```

```python
import math

import jax
import jax.numpy as jnp
from jax import lax
from jax.experimental import pallas as pl
from jax.experimental.pallas import tpu as pltpu
from jax.sharding import PartitionSpec as P

MAXDIST = 128
TILE = 128


epsilon = 1e-06
neg_large = -1e30
highest = lax.Precision.HIGHEST


def thresholds(buckets, farthest):
    exact_count = buckets // 4
    return [
        math.ceil(exact_count * (farthest / exact_count) ** (tier_index / exact_count))
        for tier_index in range(1, exact_count)
    ]


def bucket_of(distance, buckets, farthest):
    exact_count = buckets // 4
    magnitude = jnp.abs(distance)
    beyond = exact_count + sum(
        (
            (magnitude >= edge_value).astype(jnp.int32)
            for edge_value in thresholds(buckets, farthest)
        )
    )
    near_far = jnp.where(magnitude < exact_count, magnitude, beyond)
    return jnp.where(distance > 0, 2 * exact_count, 0) + near_far


def bias_buckets(buckets):
    distance = jnp.arange(4 * TILE, dtype=jnp.int32) - 2 * TILE
    return (
        bucket_of(distance, buckets, MAXDIST)[:, None]
        == jnp.arange(buckets, dtype=jnp.int32)[None, :]
    ).astype(jnp.float32)


def skew(line):
    span = line.shape[1]
    rows = lax.broadcasted_iota(jnp.int32, (8, span), 0)
    tile = jnp.broadcast_to(line, (8, span))
    for step in (1, 2, 4):
        tile = jnp.where((rows & step) != 0, pltpu.roll(tile, step, 1), tile)
    step = 8
    while step < TILE:
        tile = jnp.concatenate([tile, pltpu.roll(tile, step, 1)], axis=0)
        step *= 2
    return tile


def skew_sum(tile):
    span = tile.shape[1]
    step = TILE // 2
    while step >= 8:
        tile = tile[:step] + pltpu.roll(tile[step:], span - step, 1)
        step //= 2
    for step in (4, 2, 1):
        tile = tile + pltpu.roll(pltpu.roll(tile, span - step, 1), 8 - step, 0)
    return tile[:1]


def tile_bias(strips, along, row_tile, tiles):
    pieces = []
    for column_tile in range(tiles):
        apart = column_tile - row_tile
        if abs(apart) <= 1:
            pieces.append(strips[:, (apart + 2) * TILE : (apart + 3) * TILE])
        else:
            edge = along[:, :TILE] if apart < 0 else along[:, 3 * TILE :]
            pieces.append(jnp.broadcast_to(edge, (TILE, TILE)))
    return jnp.concatenate(pieces, axis=1)


def half_masks(width, value):
    lanes = lax.broadcasted_iota(jnp.int32, (1, width), 1)
    first = jnp.where(lanes < width // 2, value, 0.0)
    return first.astype(jnp.bfloat16), (value - first).astype(jnp.bfloat16)


def two_heads(rows, masks):
    return jnp.concatenate([rows * masks[0], rows * masks[1]], axis=0)


def dot_last(left_side, right_side):
    return lax.dot_general(
        left_side, right_side, (((1,), (1,)), ((), ())), preferred_element_type=jnp.float32
    )


def dot_plain(left_side, right_side):
    return lax.dot_general(
        left_side, right_side, (((1,), (0,)), ((), ())), preferred_element_type=jnp.float32
    )


def pair_scores(queries, keys, strips, along, seg_col, seg_row, row_tile):
    tiles = keys.shape[0] // TILE
    bias = jnp.concatenate(
        [tile_bias(strips[head], along[head], row_tile, tiles) for head in range(2)], axis=0
    )
    rows = slice(row_tile * TILE, (row_tile + 1) * TILE)
    allowed = seg_col[rows] == seg_row
    allowed = jnp.concatenate([allowed, allowed], axis=0)
    return jnp.where(allowed, dot_last(queries, keys) + bias, neg_large)


def attend_kernel(q_ref, k_ref, v_ref, seg_col_ref, seg_row_ref, along_ref, out_ref, lse_ref):
    token_rows, pair = k_ref.shape
    keys, values = k_ref[...], v_ref[...]
    seg_col, seg_row = seg_col_ref[...], seg_row_ref[...]
    along = [along_ref[0, head : head + 1, :] for head in range(2)]
    strips = [skew(line) for line in along]
    masks = half_masks(pair, 0.125)
    first = lax.broadcasted_iota(jnp.int32, (TILE, pair), 1) < pair // 2
    for row_tile in range(token_rows // TILE):
        rows = slice(row_tile * TILE, (row_tile + 1) * TILE)
        queries = two_heads(q_ref[rows, :], masks)
        scores = pair_scores(queries, keys, strips, along, seg_col, seg_row, row_tile)
        largest = jnp.max(scores, axis=-1, keepdims=True)
        exp_scores = jnp.exp(scores - largest)
        totals = jnp.sum(exp_scores, axis=-1, keepdims=True)
        weights_low = (exp_scores * (1.0 / totals)).astype(jnp.bfloat16)
        mixed = dot_plain(weights_low, values)
        out_ref[rows, :] = jnp.where(first, mixed[:TILE], mixed[TILE:]).astype(jnp.bfloat16)
        log_totals = jnp.broadcast_to(largest + jnp.log(totals), (2 * TILE, pair))
        lse_ref[rows, :] = jnp.where(first, log_totals[:TILE], log_totals[TILE:])


def attend_back_kernel(
    q_ref,
    k_ref,
    v_ref,
    seg_col_ref,
    seg_row_ref,
    along_ref,
    lse_ref,
    grad_ref,
    q_grad_ref,
    k_grad_ref,
    v_grad_ref,
    along_grad_ref,
):
    token_rows, pair = k_ref.shape
    tiles = token_rows // TILE
    keys, values = k_ref[...], v_ref[...]
    seg_col, seg_row = seg_col_ref[...], seg_row_ref[...]
    along = [along_ref[0, head : head + 1, :] for head in range(2)]
    strips = [skew(line) for line in along]
    scaled = half_masks(pair, 0.125)
    ones = half_masks(pair, 1.0)
    keys_two = two_heads(keys, scaled)
    key_total = value_total = None
    sums = {}
    for row_tile in range(tiles):
        rows = slice(row_tile * TILE, (row_tile + 1) * TILE)
        queries = two_heads(q_ref[rows, :], scaled)
        upstream = two_heads(grad_ref[rows, :], ones)
        lse_both = lse_ref[rows, :]
        log_totals = jnp.concatenate(
            [lse_both[:, :1], lse_both[:, pair // 2 : pair // 2 + 1]], axis=0
        )
        scores = pair_scores(queries, keys, strips, along, seg_col, seg_row, row_tile)
        weights_soft = jnp.exp(scores - log_totals)
        prob_grad = dot_last(upstream, values)
        weighted = weights_soft * prob_grad
        centre = jnp.sum(weighted, axis=-1, keepdims=True)
        score_grad = (weighted - weights_soft * centre).astype(jnp.bfloat16)
        weights_low = weights_soft.astype(jnp.bfloat16)
        wide = jnp.concatenate([score_grad[:TILE], score_grad[TILE:]], axis=1)
        q_grad_ref[rows, :] = dot_plain(wide, keys_two).astype(jnp.bfloat16)
        key_part = contract_rows(score_grad, queries)
        value_part = contract_rows(weights_low, upstream)
        key_total = key_part if key_total is None else key_total + key_part
        value_total = value_part if value_total is None else value_total + value_part
        score_wide = score_grad.astype(jnp.float32)
        for head in range(2):
            for column_tile in range(tiles):
                apart = max(-2, min(2, column_tile - row_tile))
                piece = score_wide[
                    head * TILE : (head + 1) * TILE,
                    column_tile * TILE : (column_tile + 1) * TILE,
                ]
                had = sums.get((head, apart))
                sums[(head, apart)] = piece if had is None else had + piece
    k_grad_ref[...] = key_total.astype(jnp.bfloat16)
    v_grad_ref[...] = value_total.astype(jnp.bfloat16)
    zero = jnp.zeros((TILE, TILE), jnp.float32)
    for head in range(2):
        strip = jnp.concatenate(
            [zero] + [sums.get((head, apart), zero) for apart in (-1, 0, 1)], axis=1
        )
        nothing = jnp.zeros((1, TILE), jnp.float32)
        below, above = (
            jnp.sum(sums.get((head, apart), zero), axis=0, keepdims=True) for apart in (-2, 2)
        )
        far = jnp.concatenate([below, nothing, nothing, above], axis=1)
        along_grad_ref[0, head : head + 1, :] = skew_sum(strip) + far


def attention_specs(token_rows, pair, pairs):
    def part(which):
        return pl.BlockSpec((token_rows, pair), lambda step: (0, which * pairs + step))

    return [
        part(0),
        part(1),
        part(2),
        pl.BlockSpec((token_rows, 1), lambda step: (0, 0)),
        pl.BlockSpec((1, token_rows), lambda step: (0, 0)),
        pl.BlockSpec((1, 2, 4 * TILE), lambda step: (step, 0, 0)),
    ]


def attend(packed, segment_ids, along):
    token_rows, width = packed.shape[0], packed.shape[1] // 3
    pairs = along.shape[0]
    pair = width // pairs
    column = pl.BlockSpec((token_rows, pair), lambda step: (0, step))
    return pl.pallas_call(
        attend_kernel,
        grid=(pairs,),
        in_specs=attention_specs(token_rows, pair, pairs),
        out_specs=[column, column],
        out_shape=[
            jax.ShapeDtypeStruct((token_rows, width), jnp.bfloat16),
            jax.ShapeDtypeStruct((token_rows, width), jnp.float32),
        ],
        compiler_params=pltpu.CompilerParams(vmem_limit_bytes=40 * 1024 * 1024),
        cost_estimate=pl.CostEstimate(
            flops=4 * token_rows * token_rows * width,
            bytes_accessed=12 * token_rows * width,
            transcendentals=2 * pairs * token_rows * token_rows,
        ),
        name="attend",
    )(packed, packed, packed, segment_ids[:, None], segment_ids[None, :], along)


def attend_back(packed, segment_ids, along, log_totals, attended_grad):
    token_rows, width = packed.shape[0], packed.shape[1] // 3
    pairs = along.shape[0]
    pair = width // pairs
    column = pl.BlockSpec((token_rows, pair), lambda step: (0, step))
    line = pl.BlockSpec((1, 2, 4 * TILE), lambda step: (step, 0, 0))
    return pl.pallas_call(
        attend_back_kernel,
        grid=(pairs,),
        in_specs=attention_specs(token_rows, pair, pairs) + [column, column],
        out_specs=[column, column, column, line],
        out_shape=[jax.ShapeDtypeStruct((token_rows, width), jnp.bfloat16)] * 3
        + [jax.ShapeDtypeStruct(along.shape, jnp.float32)],
        compiler_params=pltpu.CompilerParams(vmem_limit_bytes=40 * 1024 * 1024),
        cost_estimate=pl.CostEstimate(
            flops=10 * token_rows * token_rows * width,
            bytes_accessed=18 * token_rows * width,
            transcendentals=2 * pairs * token_rows * token_rows,
        ),
        name="attend_back",
    )(
        packed,
        packed,
        packed,
        segment_ids[:, None],
        segment_ids[None, :],
        along,
        log_totals,
        attended_grad,
    )


def normalize(values, gain):
    scale_inv = lax.rsqrt(jnp.mean(values * values, axis=-1, keepdims=True) + epsilon)
    return (values * scale_inv * gain, scale_inv)


def norm_backward(values, scale_inv, gain, upstream):
    scaled = upstream * gain
    inner_mean = jnp.mean(scaled * values, axis=-1, keepdims=True)
    grad_values = scale_inv * scaled - values * scale_inv * scale_inv * scale_inv * inner_mean
    grad_gain = jnp.sum(upstream * values * scale_inv, axis=0)
    return (grad_values, grad_gain)


def gelu_value(values):
    return 0.5 * values * (1.0 + lax.erf(values * 0.7071067811865476))


def gelu_slope(values):
    return (
        0.5 * (1.0 + lax.erf(values * 0.7071067811865476))
        + values * jnp.exp(-0.5 * values * values) * 0.3989422804014327
    )


def contract_rows(left_side, right_side):
    return lax.dot_general(
        left_side, right_side, (((0,), (0,)), ((), ())), preferred_element_type=jnp.float32
    )


def local(
    tokens,
    segment_ids,
    routes,
    slots,
    qkv_weight,
    out_weight,
    bias_table,
    norm_gain,
    ffn_gain,
    router_weight,
    expert_in,
    expert_out,
    cotangent,
):
    token_rows, width = tokens.shape
    heads_count = bias_table.shape[1]
    experts_count = router_weight.shape[1]
    capacity = 2 * token_rows // experts_count
    weight_in = expert_in[0]
    weight_out = expert_out[0]
    full_qkv, full_out = (
        lax.all_gather(qkv_weight, "shard", axis=0, tiled=True),
        lax.all_gather(out_weight, "shard", axis=0, tiled=True),
    )
    inputs = tokens.astype(jnp.float32)
    normed, scale_one = normalize(inputs, norm_gain)
    normed_low = normed.astype(jnp.bfloat16)
    packed = jnp.dot(normed_low, full_qkv, preferred_element_type=jnp.float32).astype(jnp.bfloat16)
    buckets_hot = bias_buckets(bias_table.shape[0])
    along = jnp.dot(buckets_hot, bias_table, precision=highest).T.reshape(
        heads_count // 2, 2, 4 * TILE
    )
    mixed_blocks, log_totals = attend(packed, segment_ids, along)
    branch = jnp.dot(mixed_blocks, full_out, preferred_element_type=jnp.float32)
    middle = inputs + branch
    normed_two, scale_two = normalize(middle, ffn_gain)
    logits = jnp.dot(normed_two, router_weight, precision=highest)
    router_probs = jax.nn.softmax(logits, axis=-1)
    chosen = (routes[:, None] == jnp.arange(experts_count, dtype=jnp.int32)[None, :]).astype(
        jnp.float32
    )
    gates = jnp.sum(router_probs * chosen, axis=-1)
    sent = normed_two.astype(jnp.bfloat16)
    dest_rows = routes * capacity + slots
    outgoing = (
        jnp.zeros((experts_count * capacity, width), jnp.bfloat16)
        .at[dest_rows]
        .set(sent)
        .reshape(experts_count, capacity, width)
    )
    arrived_rows = lax.all_to_all(outgoing, "expert", split_axis=0, concat_axis=0, tiled=True)
    upstream = cotangent.astype(jnp.float32)
    row_grad = (gates[:, None] * upstream).astype(jnp.bfloat16)
    grad_buffer = (
        jnp.zeros((experts_count * capacity, width), jnp.bfloat16)
        .at[dest_rows]
        .set(row_grad)
        .reshape(experts_count, capacity, width)
    )
    grad_arrived = lax.all_to_all(grad_buffer, "expert", split_axis=0, concat_axis=0, tiled=True)
    flat_in = arrived_rows.reshape(-1, width)
    inner_flat = jnp.dot(flat_in, weight_in, preferred_element_type=jnp.float32)
    activated = gelu_value(inner_flat).astype(jnp.bfloat16)
    result_rows = jnp.dot(activated, weight_out, preferred_element_type=jnp.float32).astype(
        jnp.bfloat16
    )
    result_rows, flat_grad = lax.optimization_barrier(
        (result_rows, grad_arrived.reshape(-1, width))
    )
    coming_back = lax.all_to_all(
        result_rows.reshape(arrived_rows.shape), "expert", split_axis=0, concat_axis=0, tiled=True
    ).reshape(experts_count * capacity, width)
    act_grad = jnp.dot(flat_grad, weight_out.T, preferred_element_type=jnp.float32)
    inner_grad = (act_grad * gelu_slope(inner_flat)).astype(jnp.bfloat16)
    input_grad = jnp.dot(inner_grad, weight_in.T, preferred_element_type=jnp.float32).astype(
        jnp.bfloat16
    )
    input_grad, inner_grad, activated, flat_in, flat_grad = lax.optimization_barrier(
        (input_grad, inner_grad, activated, flat_in, flat_grad)
    )
    returned_grad = lax.all_to_all(
        input_grad.reshape(arrived_rows.shape), "expert", split_axis=0, concat_axis=0, tiled=True
    ).reshape(experts_count * capacity, width)
    expert_rows = jnp.take(coming_back, dest_rows, axis=0).astype(jnp.float32)
    layer_out = middle + gates[:, None] * expert_rows
    gate_grad = jnp.sum(upstream * expert_rows, axis=-1)
    sent_grad = jnp.take(returned_grad, dest_rows, axis=0).astype(jnp.float32)
    columns = flat_in
    grad_in_rows = lax.psum_scatter(
        contract_rows(columns, inner_grad).astype(jnp.bfloat16),
        "shard",
        scatter_dimension=0,
        tiled=True,
    ).astype(jnp.float32)
    columns = activated
    grad_out_rows = lax.psum_scatter(
        contract_rows(columns, flat_grad).astype(jnp.bfloat16),
        "shard",
        scatter_dimension=0,
        tiled=True,
    ).astype(jnp.float32)
    logit_grad = (gate_grad * gates)[:, None] * (chosen - router_probs)
    router_grad = lax.dot_general(
        normed_two, logit_grad, (((0,), (0,)), ((), ())), precision=highest
    )
    normed_two_grad = jnp.dot(logit_grad, router_weight.T, precision=highest) + sent_grad
    middle_norm_grad, ffn_gain_grad = norm_backward(middle, scale_two, ffn_gain, normed_two_grad)
    middle_grad = upstream + middle_norm_grad
    branch_grad = middle_grad.astype(jnp.bfloat16)
    attended_grad = jnp.dot(branch_grad, full_out.T, preferred_element_type=jnp.float32).astype(
        jnp.bfloat16
    )
    query_grads, key_grad, value_grad, along_grad = attend_back(
        packed, segment_ids, along, log_totals, attended_grad
    )
    table_grad = lax.dot_general(
        buckets_hot,
        along_grad.reshape(heads_count, 4 * TILE),
        (((0,), (1,)), ((), ())),
        precision=highest,
    )
    packed_grad = jnp.concatenate([query_grads, key_grad, value_grad], axis=1)
    normed_grad = jnp.dot(packed_grad, full_qkv.T, preferred_element_type=jnp.float32)
    input_norm_grad, norm_gain_grad = norm_backward(inputs, scale_one, norm_gain, normed_grad)
    grad_tokens = middle_grad + input_norm_grad
    grad_qkv = lax.psum_scatter(
        contract_rows(normed_low, packed_grad).astype(jnp.bfloat16),
        ("expert", "shard"),
        scatter_dimension=0,
        tiled=True,
    ).astype(jnp.float32)
    grad_out_weight = lax.psum_scatter(
        contract_rows(mixed_blocks, branch_grad).astype(jnp.bfloat16),
        ("expert", "shard"),
        scatter_dimension=0,
        tiled=True,
    ).astype(jnp.float32)
    table_grad, norm_gain_grad, ffn_gain_grad, router_grad = lax.psum(
        (table_grad, norm_gain_grad, ffn_gain_grad, router_grad), ("expert", "shard")
    )
    return (
        layer_out,
        grad_tokens,
        grad_qkv,
        grad_out_weight,
        table_grad,
        norm_gain_grad,
        ffn_gain_grad,
        router_grad,
        grad_in_rows[None],
        grad_out_rows[None],
    )


def solution(mesh):
    placed = (
        P(("expert", "shard"), None),
        P(("expert", "shard")),
        P(("expert", "shard")),
        P(("expert", "shard")),
        P("shard", None),
        P("shard", None),
        P(),
        P(),
        P(),
        P(),
        P("expert", None, None),
        P("expert", None, None),
        P(("expert", "shard"), None),
    )
    return jax.shard_map(
        local,
        mesh=mesh,
        in_specs=placed,
        out_specs=(
            P(("expert", "shard"), None),
            P(("expert", "shard"), None),
            P(("expert", "shard"), None),
            P(("expert", "shard"), None),
            P(),
            P(),
            P(),
            P(),
            P("expert", "shard", None),
            P("expert", "shard", None),
        ),
        check_vma=False,
    )
```

```python
import math

import jax
import jax.numpy as jnp
from jax import lax
from jax.experimental import pallas as pl
from jax.experimental.pallas import tpu as pltpu
from jax.sharding import PartitionSpec as P

MAXDIST = 128
TILE = 128


epsilon = 1e-06
neg_large = -1e30
highest = lax.Precision.HIGHEST


def thresholds(buckets, farthest):
    exact_count = buckets // 4
    return [
        math.ceil(exact_count * (farthest / exact_count) ** (tier_index / exact_count))
        for tier_index in range(1, exact_count)
    ]


def bucket_of(distance, buckets, farthest):
    exact_count = buckets // 4
    magnitude = jnp.abs(distance)
    beyond = exact_count + sum(
        (
            (magnitude >= edge_value).astype(jnp.int32)
            for edge_value in thresholds(buckets, farthest)
        )
    )
    near_far = jnp.where(magnitude < exact_count, magnitude, beyond)
    return jnp.where(distance > 0, 2 * exact_count, 0) + near_far


def bias_buckets(buckets):
    distance = jnp.arange(4 * TILE, dtype=jnp.int32) - 2 * TILE
    return (
        bucket_of(distance, buckets, MAXDIST)[:, None]
        == jnp.arange(buckets, dtype=jnp.int32)[None, :]
    ).astype(jnp.float32)


def skew(line):
    span = line.shape[1]
    rows = lax.broadcasted_iota(jnp.int32, (8, span), 0)
    tile = jnp.broadcast_to(line, (8, span))
    for step in (1, 2, 4):
        tile = jnp.where((rows & step) != 0, pltpu.roll(tile, step, 1), tile)
    step = 8
    while step < TILE:
        tile = jnp.concatenate([tile, pltpu.roll(tile, step, 1)], axis=0)
        step *= 2
    return tile


def skew_sum(tile):
    span = tile.shape[1]
    step = TILE // 2
    while step >= 8:
        tile = tile[:step] + pltpu.roll(tile[step:], span - step, 1)
        step //= 2
    for step in (4, 2, 1):
        tile = tile + pltpu.roll(pltpu.roll(tile, span - step, 1), 8 - step, 0)
    return tile[:1]


def tile_bias(strips, along, row_tile, tiles):
    pieces = []
    for column_tile in range(tiles):
        apart = column_tile - row_tile
        if abs(apart) <= 1:
            pieces.append(strips[:, (apart + 2) * TILE : (apart + 3) * TILE])
        else:
            edge = along[:, :TILE] if apart < 0 else along[:, 3 * TILE :]
            pieces.append(jnp.broadcast_to(edge, (TILE, TILE)))
    return jnp.concatenate(pieces, axis=1)


def half_masks(width, value):
    lanes = lax.broadcasted_iota(jnp.int32, (1, width), 1)
    first = jnp.where(lanes < width // 2, value, 0.0)
    return first.astype(jnp.bfloat16), (value - first).astype(jnp.bfloat16)


def two_heads(rows, masks):
    return jnp.concatenate([rows * masks[0], rows * masks[1]], axis=0)


def dot_last(left_side, right_side):
    return lax.dot_general(
        left_side, right_side, (((1,), (1,)), ((), ())), preferred_element_type=jnp.float32
    )


def dot_plain(left_side, right_side):
    return lax.dot_general(
        left_side, right_side, (((1,), (0,)), ((), ())), preferred_element_type=jnp.float32
    )


def pair_scores(queries, keys, strips, along, seg_col, seg_row, row_tile):
    tiles = keys.shape[0] // TILE
    bias = jnp.concatenate(
        [tile_bias(strips[head], along[head], row_tile, tiles) for head in range(2)], axis=0
    )
    rows = slice(row_tile * TILE, (row_tile + 1) * TILE)
    allowed = seg_col[rows] == seg_row
    allowed = jnp.concatenate([allowed, allowed], axis=0)
    return jnp.where(allowed, dot_last(queries, keys) + bias, neg_large)


def attend_kernel(q_ref, k_ref, v_ref, seg_col_ref, seg_row_ref, along_ref, out_ref, lse_ref):
    token_rows, pair = k_ref.shape
    keys, values = k_ref[...], v_ref[...]
    seg_col, seg_row = seg_col_ref[...], seg_row_ref[...]
    along = [along_ref[0, head : head + 1, :] for head in range(2)]
    strips = [skew(line) for line in along]
    masks = half_masks(pair, 0.125)
    first = lax.broadcasted_iota(jnp.int32, (TILE, pair), 1) < pair // 2
    for row_tile in range(token_rows // TILE):
        rows = slice(row_tile * TILE, (row_tile + 1) * TILE)
        queries = two_heads(q_ref[rows, :], masks)
        scores = pair_scores(queries, keys, strips, along, seg_col, seg_row, row_tile)
        largest = jnp.max(scores, axis=-1, keepdims=True)
        exp_scores = jnp.exp(scores - largest)
        totals = jnp.sum(exp_scores, axis=-1, keepdims=True)
        weights_low = (exp_scores * (1.0 / totals)).astype(jnp.bfloat16)
        mixed = dot_plain(weights_low, values)
        out_ref[rows, :] = jnp.where(first, mixed[:TILE], mixed[TILE:]).astype(jnp.bfloat16)
        log_totals = jnp.broadcast_to(largest + jnp.log(totals), (2 * TILE, pair))
        lse_ref[rows, :] = jnp.where(first, log_totals[:TILE], log_totals[TILE:])


def attend_back_kernel(
    q_ref,
    k_ref,
    v_ref,
    seg_col_ref,
    seg_row_ref,
    along_ref,
    lse_ref,
    grad_ref,
    q_grad_ref,
    k_grad_ref,
    v_grad_ref,
    along_grad_ref,
):
    token_rows, pair = k_ref.shape
    tiles = token_rows // TILE
    keys, values = k_ref[...], v_ref[...]
    seg_col, seg_row = seg_col_ref[...], seg_row_ref[...]
    along = [along_ref[0, head : head + 1, :] for head in range(2)]
    strips = [skew(line) for line in along]
    scaled = half_masks(pair, 0.125)
    ones = half_masks(pair, 1.0)
    keys_two = two_heads(keys, scaled)
    key_total = value_total = None
    sums = {}
    for row_tile in range(tiles):
        rows = slice(row_tile * TILE, (row_tile + 1) * TILE)
        queries = two_heads(q_ref[rows, :], scaled)
        upstream = two_heads(grad_ref[rows, :], ones)
        lse_both = lse_ref[rows, :]
        log_totals = jnp.concatenate(
            [lse_both[:, :1], lse_both[:, pair // 2 : pair // 2 + 1]], axis=0
        )
        scores = pair_scores(queries, keys, strips, along, seg_col, seg_row, row_tile)
        weights_soft = jnp.exp(scores - log_totals)
        prob_grad = dot_last(upstream, values)
        weighted = weights_soft * prob_grad
        centre = jnp.sum(weighted, axis=-1, keepdims=True)
        score_grad = (weighted - weights_soft * centre).astype(jnp.bfloat16)
        weights_low = weights_soft.astype(jnp.bfloat16)
        wide = jnp.concatenate([score_grad[:TILE], score_grad[TILE:]], axis=1)
        q_grad_ref[rows, :] = dot_plain(wide, keys_two).astype(jnp.bfloat16)
        key_part = contract_rows(score_grad, queries)
        value_part = contract_rows(weights_low, upstream)
        key_total = key_part if key_total is None else key_total + key_part
        value_total = value_part if value_total is None else value_total + value_part
        score_wide = score_grad.astype(jnp.float32)
        for head in range(2):
            for column_tile in range(tiles):
                apart = max(-2, min(2, column_tile - row_tile))
                piece = score_wide[
                    head * TILE : (head + 1) * TILE,
                    column_tile * TILE : (column_tile + 1) * TILE,
                ]
                had = sums.get((head, apart))
                sums[(head, apart)] = piece if had is None else had + piece
    k_grad_ref[...] = key_total.astype(jnp.bfloat16)
    v_grad_ref[...] = value_total.astype(jnp.bfloat16)
    zero = jnp.zeros((TILE, TILE), jnp.float32)
    for head in range(2):
        strip = jnp.concatenate(
            [zero] + [sums.get((head, apart), zero) for apart in (-1, 0, 1)], axis=1
        )
        nothing = jnp.zeros((1, TILE), jnp.float32)
        below, above = (
            jnp.sum(sums.get((head, apart), zero), axis=0, keepdims=True) for apart in (-2, 2)
        )
        far = jnp.concatenate([below, nothing, nothing, above], axis=1)
        along_grad_ref[0, head : head + 1, :] = skew_sum(strip) + far


def attention_specs(token_rows, pair, pairs):
    def part(which):
        return pl.BlockSpec((token_rows, pair), lambda step: (0, which * pairs + step))

    return [
        part(0),
        part(1),
        part(2),
        pl.BlockSpec((token_rows, 1), lambda step: (0, 0)),
        pl.BlockSpec((1, token_rows), lambda step: (0, 0)),
        pl.BlockSpec((1, 2, 4 * TILE), lambda step: (step, 0, 0)),
    ]


def attend(packed, segment_ids, along):
    token_rows, width = packed.shape[0], packed.shape[1] // 3
    pairs = along.shape[0]
    pair = width // pairs
    column = pl.BlockSpec((token_rows, pair), lambda step: (0, step))
    return pl.pallas_call(
        attend_kernel,
        grid=(pairs,),
        in_specs=attention_specs(token_rows, pair, pairs),
        out_specs=[column, column],
        out_shape=[
            jax.ShapeDtypeStruct((token_rows, width), jnp.bfloat16),
            jax.ShapeDtypeStruct((token_rows, width), jnp.float32),
        ],
        compiler_params=pltpu.CompilerParams(vmem_limit_bytes=40 * 1024 * 1024),
        cost_estimate=pl.CostEstimate(
            flops=4 * token_rows * token_rows * width,
            bytes_accessed=12 * token_rows * width,
            transcendentals=2 * pairs * token_rows * token_rows,
        ),
        name="attend",
    )(packed, packed, packed, segment_ids[:, None], segment_ids[None, :], along)


def attend_back(packed, segment_ids, along, log_totals, attended_grad):
    token_rows, width = packed.shape[0], packed.shape[1] // 3
    pairs = along.shape[0]
    pair = width // pairs
    column = pl.BlockSpec((token_rows, pair), lambda step: (0, step))
    line = pl.BlockSpec((1, 2, 4 * TILE), lambda step: (step, 0, 0))
    return pl.pallas_call(
        attend_back_kernel,
        grid=(pairs,),
        in_specs=attention_specs(token_rows, pair, pairs) + [column, column],
        out_specs=[column, column, column, line],
        out_shape=[jax.ShapeDtypeStruct((token_rows, width), jnp.bfloat16)] * 3
        + [jax.ShapeDtypeStruct(along.shape, jnp.float32)],
        compiler_params=pltpu.CompilerParams(vmem_limit_bytes=40 * 1024 * 1024),
        cost_estimate=pl.CostEstimate(
            flops=10 * token_rows * token_rows * width,
            bytes_accessed=18 * token_rows * width,
            transcendentals=2 * pairs * token_rows * token_rows,
        ),
        name="attend_back",
    )(
        packed,
        packed,
        packed,
        segment_ids[:, None],
        segment_ids[None, :],
        along,
        log_totals,
        attended_grad,
    )


def normalize(values, gain):
    scale_inv = lax.rsqrt(jnp.mean(values * values, axis=-1, keepdims=True) + epsilon)
    return (values * scale_inv * gain, scale_inv)


def norm_backward(values, scale_inv, gain, upstream):
    scaled = upstream * gain
    inner_mean = jnp.mean(scaled * values, axis=-1, keepdims=True)
    grad_values = scale_inv * scaled - values * scale_inv * scale_inv * scale_inv * inner_mean
    grad_gain = jnp.sum(upstream * values * scale_inv, axis=0)
    return (grad_values, grad_gain)


def gelu_value(values):
    return 0.5 * values * (1.0 + lax.erf(values * 0.7071067811865476))


def gelu_slope(values):
    return (
        0.5 * (1.0 + lax.erf(values * 0.7071067811865476))
        + values * jnp.exp(-0.5 * values * values) * 0.3989422804014327
    )


def contract_rows(left_side, right_side):
    return lax.dot_general(
        left_side, right_side, (((0,), (0,)), ((), ())), preferred_element_type=jnp.float32
    )


def swap(values, axes, count, bit):
    return lax.ppermute(values, axes, [(rank, rank ^ bit) for rank in range(count)])


def gather_rows(block):
    count = lax.axis_size("shard")
    rank = lax.axis_index("shard")
    pieces = {0: block}
    for apart in sorted(range(1, count), key=lambda apart: (apart & 1, -apart)):
        if not apart & 1:
            pieces[apart] = swap(block, "shard", count, apart)
    for apart in range(1, count, 2):
        pieces[apart] = swap(pieces[apart ^ 1], "shard", count, 1)
    rows = block.shape[0]
    full = jnp.zeros((count * rows,) + block.shape[1:], block.dtype)
    for apart in range(count):
        full = lax.dynamic_update_slice_in_dim(full, pieces[apart], (rank ^ apart) * rows, axis=0)
    return full


def scatter_sum(partial):
    owners, count = lax.axis_size("expert"), lax.axis_size("shard")
    rank = lax.axis_index("shard")
    columns = partial.shape[1]
    rows = partial.shape[0] // (owners * count)
    held = partial.astype(jnp.bfloat16)
    left, bit = count, 1
    while bit < count:
        held = held.reshape(owners, left // 2, 2, rows, columns)
        side = (rank // bit) % 2
        mine = lax.dynamic_index_in_dim(held, side, axis=2, keepdims=False)
        other = lax.dynamic_index_in_dim(held, 1 - side, axis=2, keepdims=False)
        came = swap(other, "shard", count, bit)
        held = (mine.astype(jnp.float32) + came.astype(jnp.float32)).astype(jnp.bfloat16)
        left //= 2
        bit *= 2
    held = held.reshape(owners, rows, columns)
    held = lax.all_to_all(held, "expert", split_axis=0, concat_axis=0, tiled=True)
    return jnp.sum(held.astype(jnp.float32), axis=0)


def sum_everywhere(arrays):
    axes = ("expert", "shard")
    count = lax.axis_size("expert") * lax.axis_size("shard")
    flat = jnp.concatenate([values.reshape(-1, 128) for values in arrays], axis=0)
    bit = 1
    while bit < count:
        flat = flat + swap(flat, axes, count, bit)
        bit *= 2
    results, start = [], 0
    for values in arrays:
        rows = values.size // 128
        results.append(flat[start : start + rows].reshape(values.shape))
        start += rows
    return results


def local(
    tokens,
    segment_ids,
    routes,
    slots,
    qkv_weight,
    out_weight,
    bias_table,
    norm_gain,
    ffn_gain,
    router_weight,
    expert_in,
    expert_out,
    cotangent,
):
    token_rows, width = tokens.shape
    heads_count = bias_table.shape[1]
    experts_count = router_weight.shape[1]
    capacity = 2 * token_rows // experts_count
    weight_in = expert_in[0]
    weight_out = expert_out[0]
    full_qkv, full_out = gather_rows(qkv_weight), gather_rows(out_weight)
    inputs = tokens.astype(jnp.float32)
    normed, scale_one = normalize(inputs, norm_gain)
    normed_low = normed.astype(jnp.bfloat16)
    packed = jnp.dot(normed_low, full_qkv, preferred_element_type=jnp.float32).astype(jnp.bfloat16)
    buckets_hot = bias_buckets(bias_table.shape[0])
    along = jnp.dot(buckets_hot, bias_table, precision=highest).T.reshape(
        heads_count // 2, 2, 4 * TILE
    )
    mixed_blocks, log_totals = attend(packed, segment_ids, along)
    branch = jnp.dot(mixed_blocks, full_out, preferred_element_type=jnp.float32)
    middle = inputs + branch
    normed_two, scale_two = normalize(middle, ffn_gain)
    logits = jnp.dot(normed_two, router_weight, precision=highest)
    router_probs = jax.nn.softmax(logits, axis=-1)
    chosen = (routes[:, None] == jnp.arange(experts_count, dtype=jnp.int32)[None, :]).astype(
        jnp.float32
    )
    gates = jnp.sum(router_probs * chosen, axis=-1)
    sent = normed_two.astype(jnp.bfloat16)
    dest_rows = routes * capacity + slots
    outgoing = (
        jnp.zeros((experts_count * capacity, width), jnp.bfloat16)
        .at[dest_rows]
        .set(sent)
        .reshape(experts_count, capacity, width)
    )
    arrived_rows = lax.all_to_all(outgoing, "expert", split_axis=0, concat_axis=0, tiled=True)
    upstream = cotangent.astype(jnp.float32)
    row_grad = (gates[:, None] * upstream).astype(jnp.bfloat16)
    grad_buffer = (
        jnp.zeros((experts_count * capacity, width), jnp.bfloat16)
        .at[dest_rows]
        .set(row_grad)
        .reshape(experts_count, capacity, width)
    )
    grad_arrived = lax.all_to_all(grad_buffer, "expert", split_axis=0, concat_axis=0, tiled=True)
    flat_in = arrived_rows.reshape(-1, width)
    inner_flat = jnp.dot(flat_in, weight_in, preferred_element_type=jnp.float32)
    activated = gelu_value(inner_flat).astype(jnp.bfloat16)
    result_rows = jnp.dot(activated, weight_out, preferred_element_type=jnp.float32).astype(
        jnp.bfloat16
    )
    result_rows, flat_grad = lax.optimization_barrier(
        (result_rows, grad_arrived.reshape(-1, width))
    )
    coming_back = lax.all_to_all(
        result_rows.reshape(arrived_rows.shape), "expert", split_axis=0, concat_axis=0, tiled=True
    ).reshape(experts_count * capacity, width)
    act_grad = jnp.dot(flat_grad, weight_out.T, preferred_element_type=jnp.float32)
    inner_grad = (act_grad * gelu_slope(inner_flat)).astype(jnp.bfloat16)
    input_grad = jnp.dot(inner_grad, weight_in.T, preferred_element_type=jnp.float32).astype(
        jnp.bfloat16
    )
    out_partial = contract_rows(activated, flat_grad).astype(jnp.bfloat16)
    input_grad, inner_grad, flat_in, out_partial = lax.optimization_barrier(
        (input_grad, inner_grad, flat_in, out_partial)
    )
    returned_grad = lax.all_to_all(
        input_grad.reshape(arrived_rows.shape), "expert", split_axis=0, concat_axis=0, tiled=True
    ).reshape(experts_count * capacity, width)
    in_partial = contract_rows(flat_in, inner_grad).astype(jnp.bfloat16)
    returned_grad, in_partial = lax.optimization_barrier((returned_grad, in_partial))
    expert_rows = jnp.take(coming_back, dest_rows, axis=0).astype(jnp.float32)
    layer_out = middle + gates[:, None] * expert_rows
    gate_grad = jnp.sum(upstream * expert_rows, axis=-1)
    sent_grad = jnp.take(returned_grad, dest_rows, axis=0).astype(jnp.float32)
    grad_out_rows = lax.psum_scatter(out_partial, "shard", scatter_dimension=0, tiled=True)
    grad_in_rows = lax.psum_scatter(in_partial, "shard", scatter_dimension=0, tiled=True).astype(
        jnp.float32
    )
    logit_grad = (gate_grad * gates)[:, None] * (chosen - router_probs)
    router_grad = lax.dot_general(
        normed_two, logit_grad, (((0,), (0,)), ((), ())), precision=highest
    )
    normed_two_grad = jnp.dot(logit_grad, router_weight.T, precision=highest) + sent_grad
    middle_norm_grad, ffn_gain_grad = norm_backward(middle, scale_two, ffn_gain, normed_two_grad)
    middle_grad = upstream + middle_norm_grad
    branch_grad = middle_grad.astype(jnp.bfloat16)
    attended_grad = jnp.dot(branch_grad, full_out.T, preferred_element_type=jnp.float32).astype(
        jnp.bfloat16
    )
    attended_grad, grad_out_rows = lax.optimization_barrier((attended_grad, grad_out_rows))
    grad_out_rows = grad_out_rows.astype(jnp.float32)
    query_grads, key_grad, value_grad, along_grad = attend_back(
        packed, segment_ids, along, log_totals, attended_grad
    )
    table_grad = lax.dot_general(
        buckets_hot,
        along_grad.reshape(heads_count, 4 * TILE),
        (((0,), (1,)), ((), ())),
        precision=highest,
    )
    packed_grad = jnp.concatenate([query_grads, key_grad, value_grad], axis=1)
    normed_grad = jnp.dot(packed_grad, full_qkv.T, preferred_element_type=jnp.float32)
    input_norm_grad, norm_gain_grad = norm_backward(inputs, scale_one, norm_gain, normed_grad)
    grad_tokens = middle_grad + input_norm_grad
    grad_out_weight = scatter_sum(contract_rows(mixed_blocks, branch_grad))
    grad_qkv = scatter_sum(contract_rows(normed_low, packed_grad))
    table_grad, norm_gain_grad, ffn_gain_grad, router_grad = sum_everywhere(
        (table_grad, norm_gain_grad, ffn_gain_grad, router_grad)
    )
    return (
        layer_out,
        grad_tokens,
        grad_qkv,
        grad_out_weight,
        table_grad,
        norm_gain_grad,
        ffn_gain_grad,
        router_grad,
        grad_in_rows[None],
        grad_out_rows[None],
    )


def solution(mesh):
    placed = (
        P(("expert", "shard"), None),
        P(("expert", "shard")),
        P(("expert", "shard")),
        P(("expert", "shard")),
        P("shard", None),
        P("shard", None),
        P(),
        P(),
        P(),
        P(),
        P("expert", None, None),
        P("expert", None, None),
        P(("expert", "shard"), None),
    )
    return jax.shard_map(
        local,
        mesh=mesh,
        in_specs=placed,
        out_specs=(
            P(("expert", "shard"), None),
            P(("expert", "shard"), None),
            P(("expert", "shard"), None),
            P(("expert", "shard"), None),
            P(),
            P(),
            P(),
            P(),
            P("expert", "shard", None),
            P("expert", "shard", None),
        ),
        check_vma=False,
    )
```
